768 devices in a mesh: seq: 48 (over z, y_lo, core), head: 16 (over y_hi, x).
Axes of the slice: x: 4, y: 8 (y_hi: 4, y_lo: 2; y = y_hi * 2 + y_lo), z: 12, core: 2. Of those that a mesh axis runs over, the one named last changes fastest.
Arguments:
- queries: float32 [12288, 16, 256], P('seq', 'head'), may hold values from -6 to 6
- key_rows: float32 [12288, 256], P(('seq', 'head')), may hold values from -6 to 6
- value_rows: float32 [12288, 256], P(('seq', 'head')), may hold values from -6 to 6
- forward_out: float32 [12288, 16, 256], P('seq', 'head'), may hold values from -6 to 6
- out_grad: float32 [12288, 16, 256], P('seq', 'head'), may hold values from -6 to 6
- log_norm: float32 [12288, 16], P('seq', 'head'), may hold values from 6 to 9
- doc_ids: int32 [12288], P(('seq', 'head')), may hold values from 0 to 5, never falling along the last dimension, each value on 1 to 4096 neighbouring positions
Outputs:
- grad_queries: float32 [12288, 16, 256], P('seq', 'head')
- grad_keys: float32 [12288, 256], P(('seq', 'head'))
- grad_values: float32 [12288, 256], P(('seq', 'head'))
The draws below stay inside these ranges and needn't reach their ends.
Inputs may be any that keep to these rules, and one draw needn't show every extreme that they name: `doc_ids`: never falling along the tokens; each document holds 1 to 4096 tokens, one exactly 4096.
All inputs are finite; a program needn't handle non-finite values.
Results may differ from the reference program's by a relative error of at most 0.0003.
Values sent between devices are 32-bit elements; how exact they have to be, the bound alone decides.
A program may use at most 64 MiB of HBM per device.

```python
import math
import jax
import jax.numpy as jnp
import numpy as np
from jax import lax

HEAD_DIM = 256
HEADS = 16
WIN = 2048
ROWS = 256
TOKENS = 12288
DOCS = 6
DOC_MOST = 4096


def block_levels(stream_key, shape, cuts, low, top_value):
    def one(dim, parts):
        steps = jax.random.uniform(jax.random.fold_in(jax.random.fold_in(stream_key, 6), dim), (parts,), jnp.float32, low / len(cuts), top_value / len(cuts))
        return jnp.repeat(jnp.exp(steps), shape[dim] // parts).reshape((-1,) + (1,) * (len(shape) - dim - 1))

    loudness = one(*cuts[0])
    for cut in cuts[1:]:
        loudness = loudness * one(*cut)
    return loudness


def split_up(number_of, total, limit, slope):
    portions = [(1 << 20) // math.isqrt(grade ** slope) + 1 for grade in range(2, number_of + 1)]
    spare, holding = total - limit - (number_of - 1), [1] * (number_of - 1)
    while spare > 0:
        free = [i for i in range(number_of - 1) if holding[i] < limit]
        whole, budget = sum([portions[i] for i in free]), spare
        for i in free:
            more = min(limit - holding[i], max(1, budget * portions[i] // whole), spare)
            holding[i] = holding[i] + more
            spare = spare - more
    return np.array([limit] + holding)


def ragged(stream_key, number_of, total, bound, slope):
    if number_of == 2:
        one = jax.random.randint(stream_key, (), max(1, total - bound), min(bound, total - 1) + 1)
        return jnp.stack([one, total - one])
    tallies = jnp.asarray(split_up(number_of, total, bound, slope), jnp.int32)
    couples = (number_of - 1) // 2
    source_of, sink = tallies[1:1 + 2 * couples:2], tallies[2:2 + 2 * couples:2]
    margin = jnp.minimum(source_of - 1, bound - sink)
    shifted = jax.random.randint(jax.random.fold_in(stream_key, 1), (couples,), 0, 1 << 20) % (margin + 1)
    tallies = tallies.at[1:1 + 2 * couples:2].set(source_of - shifted).at[2:2 + 2 * couples:2].set(sink + shifted)
    return tallies[jax.random.permutation(jax.random.fold_in(stream_key, 2), number_of)]


def noise(stream_key, shape, spread, most, pieces=(), kind=jnp.bfloat16):
    entries = spread * jax.random.normal(stream_key, shape, jnp.float32)
    if pieces:
        entries = entries * block_levels(stream_key, shape, pieces, -0.22, 0.18)
    return jnp.clip(entries, -most, most).astype(kind)


def setup_inputs(seed: int = 0) -> dict:
    streams_of = jax.random.split(jax.random.key(seed), 8)
    return {
        "queries": noise(streams_of[0], (TOKENS, HEADS, HEAD_DIM), 1.0, 6.0, ((0, 48), (1, 16)), jnp.float32),
        "key_rows": noise(streams_of[1], (TOKENS, HEAD_DIM), 1.0, 6.0, ((0, 768),), jnp.float32),
        "value_rows": noise(streams_of[2], (TOKENS, HEAD_DIM), 1.0, 6.0, ((0, 768),), jnp.float32),
        "forward_out": noise(streams_of[3], (TOKENS, HEADS, HEAD_DIM), 1.0, 6.0, ((0, 48), (1, 16)), jnp.float32),
        "out_grad": noise(streams_of[4], (TOKENS, HEADS, HEAD_DIM), 1.0, 6.0, ((0, 48), (1, 16)), jnp.float32),
        "log_norm": jnp.clip(6.0 + 3.0 * jax.random.uniform(streams_of[5], (TOKENS, HEADS), jnp.float32) ** block_levels(streams_of[5], (TOKENS, HEADS), ((0, 48), (1, 16)), -0.2, 0.2), 6.0, 9.0),
        "doc_ids": jnp.searchsorted(jnp.cumsum(ragged(streams_of[6], DOCS, TOKENS, DOC_MOST, 1)), jnp.arange(TOKENS), side="right").astype(jnp.int32),
    }


def reference(queries, key_rows, value_rows, forward_out, out_grad, log_norm, doc_ids):
    factor = HEAD_DIM ** -0.5
    extent = WIN + ROWS
    blocks = TOKENS // ROWS
    high = lax.Precision.HIGHEST
    pad_rows = jnp.zeros((WIN, HEAD_DIM), key_rows.dtype)
    keys_pad = jnp.concatenate([pad_rows, key_rows], axis=0)
    vals_pad = jnp.concatenate([pad_rows, value_rows], axis=0)
    ids_pad = jnp.concatenate([jnp.full((WIN,), -1, jnp.int32), doc_ids.astype(jnp.int32)], axis=0)

    def advance(carry, block):
        keys_grad, vals_grad = carry
        start = (block * ROWS).astype(jnp.int32)
        query_blk = lax.dynamic_slice_in_dim(queries, start, ROWS, 0)
        out_blk = lax.dynamic_slice_in_dim(forward_out, start, ROWS, 0)
        grad_blk = lax.dynamic_slice_in_dim(out_grad, start, ROWS, 0)
        norm_blk = lax.dynamic_slice_in_dim(log_norm, start, ROWS, 0)
        query_ids = lax.dynamic_slice_in_dim(doc_ids, start, ROWS, 0)
        key_blk = lax.dynamic_slice_in_dim(keys_pad, start, extent, 0)
        val_blk = lax.dynamic_slice_in_dim(vals_pad, start, extent, 0)
        key_ids = lax.dynamic_slice_in_dim(ids_pad, start, extent, 0)
        query_pos = start + jnp.arange(ROWS, dtype=jnp.int32)
        key_pos = start - WIN + jnp.arange(extent, dtype=jnp.int32)
        distance = query_pos[:, None] - key_pos[None, :]
        allowed = (distance >= 0) & (distance < WIN) & (query_ids[:, None] == key_ids[None, :]) & (key_pos[None, :] >= 0)
        scores = jnp.einsum("rhd,kd->hrk", query_blk, key_blk, precision=high) * factor
        probs = jnp.where(allowed[None], jnp.exp(scores - norm_blk.T[:, :, None]), 0.0)
        vals_blk_grad = jnp.einsum("hrk,rhd->kd", probs, grad_blk, precision=high)
        grad_probs = jnp.einsum("rhd,kd->hrk", grad_blk, val_blk, precision=high)
        delta = jnp.sum(grad_blk * out_blk, axis=-1)
        grad_scores = probs * (grad_probs - delta.T[:, :, None])
        query_grad = jnp.einsum("hrk,kd->rhd", grad_scores, key_blk, precision=high) * factor
        keys_blk_grad = jnp.einsum("hrk,rhd->kd", grad_scores, query_blk, precision=high) * factor
        keys_grad = lax.dynamic_update_slice_in_dim(keys_grad, lax.dynamic_slice_in_dim(keys_grad, start, extent, 0) + keys_blk_grad, start, 0)
        vals_grad = lax.dynamic_update_slice_in_dim(vals_grad, lax.dynamic_slice_in_dim(vals_grad, start, extent, 0) + vals_blk_grad, start, 0)
        return (keys_grad, vals_grad), query_grad

    start_carry = (jnp.zeros_like(keys_pad), jnp.zeros_like(vals_pad))
    (keys_grad, vals_grad), query_grads = lax.scan(advance, start_carry, jnp.arange(blocks, dtype=jnp.int32))
    grad_queries = query_grads.reshape(TOKENS, HEADS, HEAD_DIM)
    return grad_queries, keys_grad[WIN:], vals_grad[WIN:]
```

```python
import functools

import jax
import jax.numpy as jnp
from jax import lax
from jax.experimental import pallas as pl
from jax.experimental.pallas import tpu as pltpu
from jax.sharding import PartitionSpec as P

MESH = pl.DeviceIdType.MESH
WIN = 2048
ROWS = 256
PIECE = 16
UNITS = 5
NY = 4
BAND = NY * PIECE
KEYS = 9 * BAND
PAD = 640
f32, bf16 = jnp.float32, jnp.bfloat16


def halves(value):
    high = value.astype(bf16)
    return high, (value - high.astype(f32)).astype(bf16)


def dot(a, b, b_dim):
    return lax.dot_general(a, b, (((1,), (b_dim,)), ((), ())), preferred_element_type=f32)


def dot3(a_high, a_low, b_high, b_low, b_dim):
    return dot(a_high, b_high, b_dim) + dot(a_high, b_low, b_dim) + dot(a_low, b_high, b_dim)


def kernel(
    q_hbm, k_hbm, v_hbm, o_hbm, g_hbm, norm_hbm, ids_hbm,
    dq_out, dk_out, dv_out,
    qb, gb, st, fwd, norm_in, ids_in, k_in, v_in,
    kbuf, vbuf, idq,
    kf, kh, kl, vh, vl, kth, ktl, idk, bias,
    qh, ql, gh, gl, sh, sl,
    acc_k, acc_v, core_k, core_v, y_k, u_k, u_v, y_v, sum_k, sum_v, dq_part, dq_in,
    in_sem, x_send, x_recv, k_send, k_recv, v_send, v_recv, c_send, c_recv, r_send, r_recv,
):
    seq, head = lax.axis_index("seq"), lax.axis_index("head")
    n_seq = lax.axis_size("seq")
    unit, core = lax.div(seq, 2), lax.rem(seq, 2)
    n_unit = n_seq // 2
    yh, x = lax.div(head, 4), lax.rem(head, 4)
    other = 1 - core

    def at_unit(d):
        return (lax.rem(unit + d + n_unit, n_unit) * 2 + core, head)

    def at_y(d):
        return (seq, lax.rem(yh + d, NY) * 4 + x)

    def at_x(d):
        return (seq, yh * 4 + lax.rem(x + d + 4, 4))

    partner = (unit * 2 + other, head)

    def send(src, dst, s_sem, r_sem, to):
        copy = pltpu.make_async_remote_copy(
            src_ref=src, dst_ref=dst, send_sem=s_sem, recv_sem=r_sem, device_id=to, device_id_type=MESH
        )
        copy.start()
        started.append(copy)
        return copy

    def landed(dst, r_sem):
        pltpu.make_async_remote_copy(
            src_ref=dst, dst_ref=dst, send_sem=r_sem, recv_sem=r_sem, device_id=partner, device_id_type=MESH
        ).wait_recv()

    started = []

    loads = [
        pltpu.make_async_copy(src, dst, in_sem.at[i])
        for i, (src, dst) in enumerate(
            (
                (q_hbm, qb.at[0]), (k_hbm, k_in), (v_hbm, v_in), (ids_hbm, ids_in),
                (g_hbm, gb.at[0]), (o_hbm, fwd), (norm_hbm, norm_in),
            )
        )
    ]
    for load in loads:
        load.start()
    barrier = pltpu.get_barrier_semaphore()
    greeted = [at_x(1), at_x(-1), at_x(2), partner]
    greeted += [at_y(d) for d in (1, 2, 3)] + [at_unit(-d) for d in (1, 2, 3, 4)]
    for device in greeted:
        pl.semaphore_signal(barrier, inc=1, device_id=device, device_id_type=MESH)

    for load in loads[:4]:
        load.wait()
    ids_row = ids_in[...].astype(f32)
    across = lax.broadcasted_iota(jnp.int32, (8, PIECE), 1)
    down = lax.broadcasted_iota(jnp.int32, (8, PIECE), 0)
    ids_low = jnp.sum(jnp.where(across == down, ids_row, 0.0), axis=1, keepdims=True)
    ids_high = jnp.sum(jnp.where(across == down + 8, ids_row, 0.0), axis=1, keepdims=True)
    lane = lax.broadcasted_iota(jnp.int32, (8, 128), 1)
    ids_tile = jnp.where(lane < 64, ids_low, ids_high)
    mine_k = kbuf.at[4, core, yh]
    mine_v = vbuf.at[4, core, yh]
    kbuf[4, core, yh, 0:16, :] = k_in[:, :128]
    kbuf[4, core, yh, 16:32, :] = k_in[:, 128:]
    kbuf[4, core, yh, 32:40, :] = ids_tile
    vbuf[4, core, yh, 0:16, :] = v_in[:, :128]
    vbuf[4, core, yh, 16:32, :] = v_in[:, 128:]
    pl.semaphore_wait(barrier, len(greeted))

    q_right = send(qb.at[0], qb.at[1], x_send.at[0], x_recv.at[0], at_x(1))
    q_left = send(qb.at[0], qb.at[2], x_send.at[1], x_recv.at[1], at_x(-1))
    for d in (1, 2, 3):
        send(mine_k, mine_k, k_send.at[d - 1], k_recv.at[4, yh], at_y(d))
    for d in (1, 2, 3, 4):
        send(mine_v, vbuf.at[4 - d, core, yh], v_send.at[d - 1], v_recv.at[4 - d, yh], at_unit(d))
    for d in (1, 2, 3):
        send(mine_v, mine_v, v_send.at[d + 3], v_recv.at[4, yh], at_y(d))

    for load in loads[4:]:
        load.wait()
    product = gb[0] * fwd[...]
    fwd[...] = product
    folded = fwd[pl.ds(0, ROWS, stride=2), :] + fwd[pl.ds(1, ROWS, stride=2), :]
    st[0, 0:1, :] = norm_in[...]
    st[0, 1:2, :] = jnp.sum(folded.T, axis=0, keepdims=True)
    st[0, 2:8, :] = jnp.zeros((6, ROWS), f32)

    def ys(d):
        return lax.rem(yh + d, NY)

    for d in (1, 2, 3):
        landed(kbuf.at[4, core, ys(d)], k_recv.at[4, ys(d)])
    for d in (1, 2, 3, 4):
        send(kbuf.at[4, core], kbuf.at[4 - d, core], k_send.at[d + 2], k_recv.at[4 - d, 0], at_unit(d))
    idq[pl.ds(x, 1)] = kbuf[4, core, :, 32:40, :][None]
    for d in (1, 2, 3):
        send(idq.at[x], idq.at[x], x_send.at[d + 9], x_recv.at[d + 9], at_x(d))
    for d in (1, 2, 3, 4):
        landed(vbuf.at[4 - d, core, yh], v_recv.at[4 - d, yh])
    for d in (1, 2, 3):
        send(
            vbuf.at[pl.ds(0, 4), core, yh], vbuf.at[pl.ds(0, 4), core, yh],
            v_send.at[d + 6], v_recv.at[5, yh], at_y(d),
        )
    q_right.wait_send()
    q_left.wait_send()
    started.remove(q_right)
    started.remove(q_left)
    send(gb.at[0], gb.at[1], x_send.at[2], x_recv.at[2], at_x(1))
    send(gb.at[0], gb.at[2], x_send.at[3], x_recv.at[3], at_x(-1))
    send(st.at[0], st.at[1], x_send.at[4], x_recv.at[4], at_x(1))
    send(st.at[0], st.at[2], x_send.at[5], x_recv.at[5], at_x(-1))
    landed(qb.at[1], x_recv.at[0])
    send(qb.at[1], qb.at[3], x_send.at[6], x_recv.at[6], at_x(1))

    for d in (1, 2, 3, 4):
        landed(kbuf.at[4 - d, core], k_recv.at[4 - d, 0])
    near = pl.ds(other, 4)
    send(kbuf.at[near, core], kbuf.at[near, core], c_send.at[0], c_recv.at[0], partner)
    for d in (1, 2, 3):
        landed(vbuf.at[4, core, ys(d)], v_recv.at[4, ys(d)])
        landed(vbuf.at[pl.ds(0, 4), core, ys(d)], v_recv.at[5, ys(d)])
    send(vbuf.at[near, core], vbuf.at[near, core], c_send.at[1], c_recv.at[1], partner)
    for d in (1, 2, 3):
        landed(idq.at[lax.rem(x + 4 - d, 4)], x_recv.at[d + 9])

    pieces = []
    for y in range(NY):
        for col in range(4):
            tile = idq[col, y]
            pieces.append(jnp.broadcast_to(tile[:, 0:1], (8, 128)))
            pieces.append(jnp.broadcast_to(tile[:, 64:65], (8, 128)))
    ids_query = jnp.concatenate(pieces, axis=0).T[0:1, :]
    landed(kbuf.at[pl.ds(core, 4), other], c_recv.at[0])
    landed(vbuf.at[pl.ds(core, 4), other], c_recv.at[1])

    query_pos = core * ROWS + lax.broadcasted_iota(jnp.int32, (1, ROWS), 1)
    first = unit * 2 * ROWS

    def prepare(n, carry):
        block = core + n // NY
        y = n % NY
        j, c = lax.div(block, 2), lax.rem(block, 2)
        rows = pl.ds(pl.multiple_of(n * PIECE, PIECE), PIECE)
        keys = jnp.concatenate([kbuf[j, c, y, 0:16, :], kbuf[j, c, y, 16:32, :]], axis=1)
        vals = jnp.concatenate([vbuf[j, c, y, 0:16, :], vbuf[j, c, y, 16:32, :]], axis=1)
        kf[rows, :] = keys
        kh[rows, :], kl[rows, :] = halves(keys)
        vh[rows, :], vl[rows, :] = halves(vals)
        tile = kbuf[j, c, y, 32:40, :]
        ids = jnp.concatenate([tile[:, 0:1], tile[:, 64:65]], axis=0)
        key_pos = (block - 8) * ROWS + y * BAND + x * PIECE
        key_pos = key_pos + lax.broadcasted_iota(jnp.int32, (PIECE, ROWS), 0)
        apart = query_pos - key_pos
        allowed = (apart >= 0) & (apart < WIN) & (ids == ids_query) & (key_pos + first >= 0)
        bias[rows, :] = jnp.where(allowed, 0.0, -1e30)
        return carry

    lax.fori_loop(0, KEYS // PIECE, prepare, 0)
    kf[KEYS:PAD, :] = jnp.zeros((PAD - KEYS, 256), f32)
    sh[KEYS:PAD, :] = jnp.zeros((PAD - KEYS, ROWS), bf16)
    sl[KEYS:PAD, :] = jnp.zeros((PAD - KEYS, ROWS), bf16)
    for i in range(PAD // 128):
        cols = slice(i * 128, (i + 1) * 128)
        kth[:, cols], ktl[:, cols] = halves(kf[cols, :].T)

    TILE = 192

    def one_head(slot, is_first):
        even, odd = pl.ds(0, ROWS, stride=2), pl.ds(1, ROWS, stride=2)
        qh[...], ql[...] = halves(jnp.concatenate([qb[slot, even, :], qb[slot, odd, :]], axis=1) * 0.0625)
        gh[...], gl[...] = halves(jnp.concatenate([gb[slot, even, :], gb[slot, odd, :]], axis=1))
        norm, delta = st[slot, 0:1, :], st[slot, 1:2, :]
        for t in range(KEYS // TILE):
            rows = slice(t * TILE, (t + 1) * TILE)
            scores = dot3(kh[rows, :], kl[rows, :], qh[...], ql[...], 1)
            grads = dot3(vh[rows, :], vl[rows, :], gh[...], gl[...], 1)
            probs = jnp.exp(scores - norm + bias[rows, :])
            grads = probs * (grads - delta)
            p_high, p_low = halves(probs)
            s_high, s_low = halves(grads)
            sh[rows, :] = s_high
            sl[rows, :] = s_low
            out = pl.ds(pl.multiple_of(core * BAND + t * TILE, BAND), TILE)
            part_v = dot3(p_high, p_low, gh[...], gl[...], 0)
            part_k = dot3(s_high, s_low, qh[...], ql[...], 0)
            if is_first:
                acc_v[out, :] = part_v
                acc_k[out, :] = part_k
            else:
                acc_v[out, :] += part_v
                acc_k[out, :] += part_k
        dq_part[slot] = dot3(kth[...], ktl[...], sh[...], sl[...], 0)

    one_head(0, True)
    landed(gb.at[2], x_recv.at[3])
    send(gb.at[2], gb.at[3], x_send.at[7], x_recv.at[7], at_x(-1))
    landed(gb.at[1], x_recv.at[2])
    landed(st.at[1], x_recv.at[4])
    send(st.at[1], st.at[3], x_send.at[8], x_recv.at[8], at_x(1))
    one_head(1, False)
    send(dq_part.at[1], dq_in.at[0], x_send.at[13], x_recv.at[13], at_x(-1))
    landed(qb.at[2], x_recv.at[1])
    landed(st.at[2], x_recv.at[5])
    one_head(2, False)
    send(dq_part.at[2], dq_in.at[1], x_send.at[14], x_recv.at[14], at_x(1))
    landed(qb.at[3], x_recv.at[6])
    landed(gb.at[3], x_recv.at[7])
    landed(st.at[3], x_recv.at[8])
    one_head(3, False)
    send(dq_part.at[3], dq_in.at[2], x_send.at[15], x_recv.at[15], at_x(2))

    def band(ref, j, c):
        return ref.at[pl.ds(pl.multiple_of((j * 2 + c) * BAND, BAND), BAND)]

    def rows_of(j, c, y=0, count=BAND):
        return pl.ds(pl.multiple_of((j * 2 + c) * BAND + y * PIECE, PIECE), count)

    for i in range(4):
        j = core + i
        send(band(acc_v, j, other), core_v.at[i], c_send.at[2 + i], c_recv.at[2 + i], partner)
        send(band(acc_k, j, other), core_k.at[i], c_send.at[6 + i], c_recv.at[6 + i], partner)
    for i in range(4):
        j = other + i
        landed(core_v.at[i], c_recv.at[2 + i])
        acc_v[rows_of(j, core), :] += core_v[i]
    for d in (1, 2, 3, 4):
        send(band(acc_v, 4 - d, core), u_v.at[d - 1], r_send.at[d - 1], r_recv.at[d - 1], at_unit(-d))
    for i in range(4):
        j = other + i
        landed(core_k.at[i], c_recv.at[6 + i])
        acc_k[rows_of(j, core), :] += core_k[i]
    for d in (1, 2, 3):
        y = ys(d)
        for j in range(UNITS):
            sum_k[d, j] = acc_k[rows_of(j, core, y, PIECE), :]
        send(sum_k.at[d], y_k.at[d - 1], r_send.at[d + 3], r_recv.at[d + 3], at_y(d))

    total = acc_v[rows_of(4, core), :]
    for d in (1, 2, 3, 4):
        landed(u_v.at[d - 1], r_recv.at[d - 1])
        total = total + u_v[d - 1]
    sum_v[...] = total
    for d in (1, 2, 3):
        src = sum_v.at[pl.ds(pl.multiple_of(ys(d) * PIECE, PIECE), PIECE)]
        send(src, y_v.at[d - 1], r_send.at[d + 6], r_recv.at[d + 6], at_y(d))
    for d in (1, 2, 3):
        landed(y_k.at[d - 1], r_recv.at[d + 3])
    for j in range(UNITS):
        sum_k[0, j] = acc_k[rows_of(j, core, yh, PIECE), :] + y_k[0, j] + y_k[1, j] + y_k[2, j]
    for d in (1, 2, 3, 4):
        send(sum_k.at[0, 4 - d], u_k.at[d - 1], r_send.at[d + 9], r_recv.at[d + 9], at_unit(-d))

    for i in range(3):
        landed(dq_in.at[i], x_recv.at[13 + i])
    total_q = (dq_part[0] + dq_in[0] + dq_in[1] + dq_in[2]) * 0.0625
    total_q = total_q.T
    dq_out[pl.ds(0, ROWS, stride=2), :] = total_q[:, :128]
    dq_out[pl.ds(1, ROWS, stride=2), :] = total_q[:, 128:]

    total = sum_v[pl.ds(pl.multiple_of(yh * PIECE, PIECE), PIECE), :]
    for d in (1, 2, 3):
        landed(y_v.at[d - 1], r_recv.at[d + 6])
        total = total + y_v[d - 1]
    dv_out[...] = total
    total = sum_k[0, 4]
    for d in (1, 2, 3, 4):
        landed(u_k.at[d - 1], r_recv.at[d + 9])
        total = total + u_k[d - 1]
    dk_out[...] = total
    for copy in started:
        copy.wait_send()


def on_device(queries, key_rows, value_rows, forward_out, out_grad, log_norm, doc_ids):
    flat = (2 * ROWS, 128)
    vmem, dma = pltpu.VMEM, pltpu.SemaphoreType.DMA
    dq, dk, dv = pl.pallas_call(
        kernel,
        out_shape=(
            jax.ShapeDtypeStruct(flat, f32),
            jax.ShapeDtypeStruct((PIECE, 256), f32),
            jax.ShapeDtypeStruct((PIECE, 256), f32),
        ),
        in_specs=[pl.BlockSpec(memory_space=pl.ANY)] * 7,
        out_specs=(pl.BlockSpec(memory_space=pltpu.VMEM),) * 3,
        scratch_shapes=[
            vmem((4, *flat), f32), vmem((4, *flat), f32), vmem((4, 8, ROWS), f32), vmem(flat, f32),
            vmem((1, ROWS), f32), vmem((1, PIECE), jnp.int32), vmem((PIECE, 256), f32), vmem((PIECE, 256), f32),
            vmem((UNITS, 2, NY, 40, 128), f32), vmem((UNITS, 2, NY, 32, 128), f32), vmem((4, NY, 8, 128), f32),
            vmem((PAD, 256), f32), vmem((KEYS, 256), bf16), vmem((KEYS, 256), bf16),
            vmem((KEYS, 256), bf16), vmem((KEYS, 256), bf16), vmem((256, PAD), bf16), vmem((256, PAD), bf16),
            vmem((8, 128), f32), vmem((KEYS, ROWS), f32),
            vmem((ROWS, 256), bf16), vmem((ROWS, 256), bf16), vmem((ROWS, 256), bf16), vmem((ROWS, 256), bf16),
            vmem((PAD, ROWS), bf16), vmem((PAD, ROWS), bf16),
            vmem((10 * BAND, 256), f32), vmem((10 * BAND, 256), f32),
            vmem((4, BAND, 256), f32), vmem((4, BAND, 256), f32),
            vmem((3, UNITS, PIECE, 256), f32), vmem((4, PIECE, 256), f32), vmem((4, BAND, 256), f32),
            vmem((3, PIECE, 256), f32), vmem((4, UNITS, PIECE, 256), f32), vmem((BAND, 256), f32),
            vmem((4, 256, ROWS), f32), vmem((3, 256, ROWS), f32),
            dma((7,)), dma((16,)), dma((16,)), dma((7,)), dma((5, NY)), dma((10,)), dma((6, NY)),
            dma((10,)), dma((10,)), dma((14,)), dma((14,)),
        ],
        compiler_params=pltpu.CompilerParams(
            collective_id=0, has_side_effects=True, vmem_limit_bytes=60 * 2**20
        ),
    )(
        queries.reshape(flat), key_rows, value_rows, forward_out.reshape(flat), out_grad.reshape(flat),
        log_norm.reshape(1, ROWS), doc_ids.reshape(1, PIECE),
    )
    return dq.reshape(ROWS, 1, 256), dk, dv


def solution(mesh):
    in_specs = (
        P("seq", "head", None),
        P(("seq", "head"), None),
        P(("seq", "head"), None),
        P("seq", "head", None),
        P("seq", "head", None),
        P("seq", "head"),
        P(("seq", "head")),
    )
    out_specs = (P("seq", "head", None), P(("seq", "head"), None), P(("seq", "head"), None))
    return jax.shard_map(
        on_device, mesh=mesh, in_specs=in_specs, out_specs=out_specs, check_vma=False
    )
```

```python
import functools

import jax
import jax.numpy as jnp
from jax import lax
from jax.experimental import pallas as pl
from jax.experimental.pallas import tpu as pltpu
from jax.sharding import PartitionSpec as P

MESH = pl.DeviceIdType.MESH
WIN = 2048
ROWS = 256
PIECE = 16
UNITS = 5
NY = 4
BAND = NY * PIECE
KEYS = 9 * BAND
PAD = 640
f32, bf16 = jnp.float32, jnp.bfloat16


def halves(value):
    high = value.astype(bf16)
    return high, (value - high.astype(f32)).astype(bf16)


def dot(a, b, b_dim):
    return lax.dot_general(a, b, (((1,), (b_dim,)), ((), ())), preferred_element_type=f32)


def dot3(a_high, a_low, b_high, b_low, b_dim):
    return dot(a_high, b_high, b_dim) + dot(a_high, b_low, b_dim) + dot(a_low, b_high, b_dim)


def kernel(
    q_hbm, k_hbm, v_hbm, o_hbm, g_hbm, norm_hbm, ids_hbm,
    dq_hbm, dk_hbm, dv_hbm,
    dq_out, dk_out, dv_out, qb, gb, st, fwd, norm_in, ids_in, k_in, v_in,
    kbuf, vbuf, idq,
    kf, kh, kl, vh, vl, kth, ktl, bias,
    qh, ql, gh, gl, sh, sl,
    acc_k, acc_v, core_k, core_v, y_k, u_k, u_v, y_v, sum_k, sum_v, dq_part, dq_in,
    in_sem, out_sem, x_send, x_recv, k_send, k_recv, v_send, v_recv, c_send, c_recv, r_send, r_recv,
):
    seq, head = lax.axis_index("seq"), lax.axis_index("head")
    n_seq = lax.axis_size("seq")
    unit, core = lax.div(seq, 2), lax.rem(seq, 2)
    n_unit = n_seq // 2
    yh, x = lax.div(head, 4), lax.rem(head, 4)
    other = 1 - core

    def at_unit(d):
        return (lax.rem(unit + d + n_unit, n_unit) * 2 + core, head)

    def at_y(d):
        return (seq, lax.rem(yh + d, NY) * 4 + x)

    def at_x(d):
        return (seq, yh * 4 + lax.rem(x + d + 4, 4))

    partner = (unit * 2 + other, head)

    def send(src, dst, s_sem, r_sem, to):
        copy = pltpu.make_async_remote_copy(
            src_ref=src, dst_ref=dst, send_sem=s_sem, recv_sem=r_sem, device_id=to, device_id_type=MESH
        )
        copy.start()
        started.append(copy)
        return copy

    def landed(dst, r_sem):
        pltpu.make_async_remote_copy(
            src_ref=dst, dst_ref=dst, send_sem=r_sem, recv_sem=r_sem, device_id=partner, device_id_type=MESH
        ).wait_recv()

    started = []

    loads = [
        pltpu.make_async_copy(src, dst, in_sem.at[i])
        for i, (src, dst) in enumerate(
            (
                (q_hbm, qb.at[0]), (k_hbm, k_in), (v_hbm, v_in), (ids_hbm, ids_in),
                (g_hbm, gb.at[0]), (o_hbm, fwd), (norm_hbm, norm_in),
            )
        )
    ]
    for load in loads:
        load.start()
    barrier = pltpu.get_barrier_semaphore()
    greeted = [at_x(1), at_x(-1), at_x(2), partner]
    greeted += [at_y(d) for d in (1, 2, 3)] + [at_unit(-d) for d in (1, 2, 3, 4)]
    for device in greeted:
        pl.semaphore_signal(barrier, inc=1, device_id=device, device_id_type=MESH)

    for load in loads[:4]:
        load.wait()
    ids_row = ids_in[...].astype(f32)
    across = lax.broadcasted_iota(jnp.int32, (8, PIECE), 1)
    down = lax.broadcasted_iota(jnp.int32, (8, PIECE), 0)
    ids_low = jnp.sum(jnp.where(across == down, ids_row, 0.0), axis=1, keepdims=True)
    ids_high = jnp.sum(jnp.where(across == down + 8, ids_row, 0.0), axis=1, keepdims=True)
    lane = lax.broadcasted_iota(jnp.int32, (8, 128), 1)
    ids_tile = jnp.where(lane < 64, ids_low, ids_high)
    mine_k = kbuf.at[4, core, 0]
    mine_v = vbuf.at[4, core, 0]
    kbuf[4, core, 0, 0:16, :] = k_in[:, :128]
    kbuf[4, core, 0, 16:32, :] = k_in[:, 128:]
    kbuf[4, core, 0, 32:40, :] = ids_tile
    vbuf[4, core, 0, 0:16, :] = v_in[:, :128]
    vbuf[4, core, 0, 16:32, :] = v_in[:, 128:]
    pl.semaphore_wait(barrier, len(greeted))

    q_right = send(qb.at[0], qb.at[1], x_send.at[0], x_recv.at[0], at_x(1))
    q_left = send(qb.at[0], qb.at[2], x_send.at[1], x_recv.at[1], at_x(-1))
    for d in (1, 2, 3):
        send(mine_k, kbuf.at[4, core, 4 - d], k_send.at[d - 1], k_recv.at[3 - d], at_y(d))
    for d in (1, 2, 3, 4):
        send(mine_v, vbuf.at[4 - d, core, 0], v_send.at[d - 1], v_recv.at[d - 1], at_unit(d))
    for d in (1, 2, 3, 4):
        send(mine_k, kbuf.at[4 - d, core, 0], k_send.at[d + 2], k_recv.at[d + 2], at_unit(d))
    for d in (1, 2, 3):
        send(mine_v, vbuf.at[4, core, 4 - d], v_send.at[d + 3], v_recv.at[d + 3], at_y(d))

    for load in loads[4:]:
        load.wait()
    product = gb[0] * fwd[...]
    fwd[...] = product
    folded = fwd[pl.ds(0, ROWS, stride=2), :] + fwd[pl.ds(1, ROWS, stride=2), :]
    st[0, 0:1, :] = norm_in[...]
    st[0, 1:2, :] = jnp.sum(folded.T, axis=0, keepdims=True)
    st[0, 2:8, :] = jnp.zeros((6, ROWS), f32)

    for r in (1, 2, 3):
        landed(kbuf.at[4, core, r], k_recv.at[r - 1])
    along = pl.ds(1, 3)
    for d in (1, 2, 3, 4):
        send(kbuf.at[4, core, along], kbuf.at[4 - d, core, along], k_send.at[d + 6], k_recv.at[d + 6], at_unit(d))
    for d in (1, 2, 3, 4):
        landed(vbuf.at[4 - d, core, 0], v_recv.at[d - 1])
    past = pl.ds(0, 4)
    for d in (1, 2, 3):
        send(vbuf.at[past, core, 0], vbuf.at[past, core, 4 - d], v_send.at[d + 6], v_recv.at[d + 6], at_y(d))
    idq[pl.ds(x, 1)] = kbuf[4, core, :, 32:40, :][None]
    for d in (1, 2, 3):
        send(idq.at[x], idq.at[x], x_send.at[d + 9], x_recv.at[d + 9], at_x(d))
    q_right.wait_send()
    q_left.wait_send()
    started.remove(q_right)
    started.remove(q_left)
    send(gb.at[0], gb.at[1], x_send.at[2], x_recv.at[2], at_x(1))
    send(gb.at[0], gb.at[2], x_send.at[3], x_recv.at[3], at_x(-1))
    send(st.at[0], st.at[1], x_send.at[4], x_recv.at[4], at_x(1))
    send(st.at[0], st.at[2], x_send.at[5], x_recv.at[5], at_x(-1))
    landed(qb.at[1], x_recv.at[0])
    send(qb.at[1], qb.at[3], x_send.at[6], x_recv.at[6], at_x(1))

    for d in (1, 2, 3):
        landed(idq.at[lax.rem(x + 4 - d, 4)], x_recv.at[d + 9])
    pieces = []
    for y in range(NY):
        for col in range(4):
            tile = idq[col, lax.rem(y + NY - yh, NY)]
            pieces.append(jnp.broadcast_to(tile[:, 0:1], (8, 128)))
            pieces.append(jnp.broadcast_to(tile[:, 64:65], (8, 128)))
    ids_query = jnp.concatenate(pieces, axis=0).T[0:1, :]
    query_pos = core * ROWS + lax.broadcasted_iota(jnp.int32, (1, ROWS), 1)
    first = unit * 2 * ROWS
    row = lax.broadcasted_iota(jnp.int32, (BAND, 1), 0)
    row_pos = lax.rem(yh + row // PIECE, NY) * BAND + x * PIECE + row % PIECE

    def prepare(band, j, c):
        rows = slice(band * BAND, (band + 1) * BAND)

        def wide(ref, lo):
            return ref[j, c, :, lo : lo + PIECE, :].reshape(BAND, 128)

        keys = jnp.concatenate([wide(kbuf, 0), wide(kbuf, PIECE)], axis=1)
        vals = jnp.concatenate([wide(vbuf, 0), wide(vbuf, PIECE)], axis=1)
        kf[rows, :] = keys
        kh[rows, :], kl[rows, :] = halves(keys)
        vh[rows, :], vl[rows, :] = halves(vals)
        tiles = kbuf[j, c, :, 32:40, :]
        ids = jnp.concatenate([tiles[:, :, 0:1], tiles[:, :, 64:65]], axis=1).reshape(BAND, 1)
        key_pos = row_pos + (core + band - 8) * ROWS
        apart = query_pos - key_pos
        allowed = (apart >= 0) & (apart < WIN) & (ids == ids_query) & (key_pos + first >= 0)
        bias[rows, :] = jnp.where(allowed, 0.0, -1e30)

    kf[KEYS:PAD, :] = jnp.zeros((PAD - KEYS, 256), f32)
    sh[KEYS:PAD, :] = jnp.zeros((PAD - KEYS, ROWS), bf16)
    sl[KEYS:PAD, :] = jnp.zeros((PAD - KEYS, ROWS), bf16)

    near = pl.ds(other, 4)
    for d in (1, 2, 3):
        landed(vbuf.at[4, core, 4 - d], v_recv.at[d + 3])
        landed(vbuf.at[past, core, 4 - d], v_recv.at[d + 6])
    send(vbuf.at[near, core], vbuf.at[near, core], c_send.at[1], c_recv.at[1], partner)
    for d in (1, 2, 3, 4):
        landed(kbuf.at[4 - d, core, 0], k_recv.at[d + 2])
        landed(kbuf.at[4 - d, core, along], k_recv.at[d + 6])
    send(kbuf.at[near, core], kbuf.at[near, core], c_send.at[0], c_recv.at[0], partner)
    for j in range(UNITS):
        prepare(2 * j, j, core)
    landed(gb.at[2], x_recv.at[3])
    send(gb.at[2], gb.at[3], x_send.at[7], x_recv.at[7], at_x(-1))
    landed(st.at[1], x_recv.at[4])
    send(st.at[1], st.at[3], x_send.at[8], x_recv.at[8], at_x(1))
    landed(vbuf.at[pl.ds(core, 4), other], c_recv.at[1])
    landed(kbuf.at[pl.ds(core, 4), other], c_recv.at[0])
    for i in range(4):
        prepare(2 * i + 1, core + i, other)
    for i in range(PAD // 128):
        cols = slice(i * 128, (i + 1) * 128)
        kth[:, cols], ktl[:, cols] = halves(kf[cols, :].T)

    TILE = 192

    def one_head(slot, is_first):
        even, odd = pl.ds(0, ROWS, stride=2), pl.ds(1, ROWS, stride=2)
        qh[...], ql[...] = halves(jnp.concatenate([qb[slot, even, :], qb[slot, odd, :]], axis=1) * 0.0625)
        gh[...], gl[...] = halves(jnp.concatenate([gb[slot, even, :], gb[slot, odd, :]], axis=1))
        norm, delta = st[slot, 0:1, :], st[slot, 1:2, :]
        for t in range(KEYS // TILE):
            rows = slice(t * TILE, (t + 1) * TILE)
            scores = dot3(kh[rows, :], kl[rows, :], qh[...], ql[...], 1)
            grads = dot3(vh[rows, :], vl[rows, :], gh[...], gl[...], 1)
            probs = jnp.exp(scores - norm + bias[rows, :])
            grads = probs * (grads - delta)
            p_high, p_low = halves(probs)
            s_high, s_low = halves(grads)
            sh[rows, :] = s_high
            sl[rows, :] = s_low
            part_v = dot3(p_high, p_low, gh[...], gl[...], 0)
            part_k = dot3(s_high, s_low, qh[...], ql[...], 0)
            for i in range(TILE // BAND):
                block = core + t * (TILE // BAND) + i
                j, c = lax.div(block, 2), lax.rem(block, 2)
                part = slice(i * BAND, (i + 1) * BAND)
                if is_first:
                    acc_v[j, c] = part_v[part]
                    acc_k[j, c] = part_k[part]
                else:
                    acc_v[j, c] += part_v[part]
                    acc_k[j, c] += part_k[part]
        dq_part[slot] = dot3(kth[...], ktl[...], sh[...], sl[...], 0)

    one_head(0, True)
    landed(gb.at[1], x_recv.at[2])
    one_head(1, False)
    send(dq_part.at[1], dq_in.at[0], x_send.at[13], x_recv.at[13], at_x(-1))
    landed(qb.at[2], x_recv.at[1])
    landed(st.at[2], x_recv.at[5])
    one_head(2, False)
    send(dq_part.at[2], dq_in.at[1], x_send.at[14], x_recv.at[14], at_x(1))
    landed(qb.at[3], x_recv.at[6])
    landed(gb.at[3], x_recv.at[7])
    landed(st.at[3], x_recv.at[8])
    one_head(3, False)

    share = pl.ds(core, 4)
    send(acc_v.at[share, other], core_v, c_send.at[2], c_recv.at[2], partner)
    send(acc_k.at[share, other], core_k, c_send.at[3], c_recv.at[3], partner)
    send(dq_part.at[3], dq_in.at[2], x_send.at[15], x_recv.at[15], at_x(2))
    landed(core_v, c_recv.at[2])
    for i in range(4):
        acc_v[other + i, core] += core_v[i]
    for d in (4, 3, 2, 1):
        send(acc_v.at[4 - d, core], u_v.at[d - 1], r_send.at[d - 1], r_recv.at[d - 1], at_unit(-d))
    landed(core_k, c_recv.at[3])
    for i in range(4):
        acc_k[other + i, core] += core_k[i]
    for r in (2, 1, 3):
        src = acc_k.at[:, core, pl.ds(r * PIECE, PIECE)]
        send(src, y_k.at[r - 1], r_send.at[r + 3], r_recv.at[r + 3], at_y(r))

    total = acc_v[4, core]
    for d in (1, 2, 3, 4):
        landed(u_v.at[d - 1], r_recv.at[d - 1])
        total = total + u_v[d - 1]
    sum_v[...] = total
    for r in (2, 1, 3):
        src = sum_v.at[pl.ds(r * PIECE, PIECE)]
        send(src, y_v.at[r - 1], r_send.at[r + 6], r_recv.at[r + 6], at_y(r))
    for r in (1, 2, 3):
        landed(y_k.at[r - 1], r_recv.at[r + 3])
    for j in range(UNITS):
        sum_k[j] = acc_k[j, core, :PIECE] + y_k[0, j] + y_k[1, j] + y_k[2, j]
    for d in (4, 3, 2, 1):
        send(sum_k.at[4 - d], u_k.at[d - 1], r_send.at[d + 9], r_recv.at[d + 9], at_unit(-d))

    for i in range(3):
        landed(dq_in.at[i], x_recv.at[13 + i])
    total_q = (dq_part[0] + dq_in[0] + dq_in[1] + dq_in[2]) * 0.0625
    total_q = total_q.T
    dq_out[pl.ds(0, ROWS, stride=2), :] = total_q[:, :128]
    dq_out[pl.ds(1, ROWS, stride=2), :] = total_q[:, 128:]
    stores = [pltpu.make_async_copy(dq_out, dq_hbm, out_sem.at[0])]
    stores[0].start()

    total = sum_v[:PIECE, :]
    for r in (1, 2, 3):
        landed(y_v.at[r - 1], r_recv.at[r + 6])
        total = total + y_v[r - 1]
    dv_out[...] = total
    stores.append(pltpu.make_async_copy(dv_out, dv_hbm, out_sem.at[1]))
    stores[1].start()
    total = sum_k[4]
    for d in (1, 2, 3, 4):
        landed(u_k.at[d - 1], r_recv.at[d + 9])
        total = total + u_k[d - 1]
    dk_out[...] = total
    stores.append(pltpu.make_async_copy(dk_out, dk_hbm, out_sem.at[2]))
    stores[2].start()
    for store in stores:
        store.wait()
    for copy in started:
        copy.wait_send()


def hand_over(dq_in, dk_in, dv_in, dq_out, dk_out, dv_out):
    dq_out[...] = dq_in[...]
    dk_out[...] = dk_in[...]
    dv_out[...] = dv_in[...]


def on_device(queries, key_rows, value_rows, forward_out, out_grad, log_norm, doc_ids):
    flat = (2 * ROWS, 128)
    vmem, dma = pltpu.VMEM, pltpu.SemaphoreType.DMA
    dq, dk, dv = pl.pallas_call(
        kernel,
        out_shape=(
            jax.ShapeDtypeStruct(flat, f32),
            jax.ShapeDtypeStruct((PIECE, 256), f32),
            jax.ShapeDtypeStruct((PIECE, 256), f32),
        ),
        in_specs=[pl.BlockSpec(memory_space=pl.ANY)] * 7,
        out_specs=(pl.BlockSpec(memory_space=pl.ANY),) * 3,
        scratch_shapes=[
            vmem(flat, f32), vmem((PIECE, 256), f32), vmem((PIECE, 256), f32),
            vmem((4, *flat), f32), vmem((4, *flat), f32), vmem((4, 8, ROWS), f32), vmem(flat, f32),
            vmem((1, ROWS), f32), vmem((1, PIECE), jnp.int32), vmem((PIECE, 256), f32), vmem((PIECE, 256), f32),
            vmem((UNITS, 2, NY, 40, 128), f32), vmem((UNITS, 2, NY, 32, 128), f32), vmem((4, NY, 8, 128), f32),
            vmem((PAD, 256), f32), vmem((KEYS, 256), bf16), vmem((KEYS, 256), bf16),
            vmem((KEYS, 256), bf16), vmem((KEYS, 256), bf16), vmem((256, PAD), bf16), vmem((256, PAD), bf16),
            vmem((KEYS, ROWS), f32),
            vmem((ROWS, 256), bf16), vmem((ROWS, 256), bf16), vmem((ROWS, 256), bf16), vmem((ROWS, 256), bf16),
            vmem((PAD, ROWS), bf16), vmem((PAD, ROWS), bf16),
            vmem((UNITS, 2, BAND, 256), f32), vmem((UNITS, 2, BAND, 256), f32),
            vmem((4, BAND, 256), f32), vmem((4, BAND, 256), f32),
            vmem((3, UNITS, PIECE, 256), f32), vmem((4, PIECE, 256), f32), vmem((4, BAND, 256), f32),
            vmem((3, PIECE, 256), f32), vmem((UNITS, PIECE, 256), f32), vmem((BAND, 256), f32),
            vmem((4, 256, ROWS), f32), vmem((3, 256, ROWS), f32),
            dma((7,)), dma((3,)), dma((16,)), dma((16,)), dma((11,)), dma((11,)), dma((10,)), dma((10,)),
            dma((4,)), dma((4,)), dma((14,)), dma((14,)),
        ],
        compiler_params=pltpu.CompilerParams(
            collective_id=0, has_side_effects=True, vmem_limit_bytes=60 * 2**20
        ),
    )(
        queries.reshape(flat), key_rows, value_rows, forward_out.reshape(flat), out_grad.reshape(flat),
        log_norm.reshape(1, ROWS), doc_ids.reshape(1, PIECE),
    )
    dq, dk, dv = pl.pallas_call(
        hand_over,
        out_shape=tuple(jax.ShapeDtypeStruct(a.shape, a.dtype) for a in (dq, dk, dv)),
        in_specs=[pl.BlockSpec(memory_space=pltpu.VMEM)] * 3,
        out_specs=(pl.BlockSpec(memory_space=pltpu.VMEM),) * 3,
    )(dq, dk, dv)
    return dq.reshape(ROWS, 1, 256), dk, dv


def solution(mesh):
    in_specs = (
        P("seq", "head", None),
        P(("seq", "head"), None),
        P(("seq", "head"), None),
        P("seq", "head", None),
        P("seq", "head", None),
        P("seq", "head"),
        P(("seq", "head")),
    )
    out_specs = (P("seq", "head", None), P(("seq", "head"), None), P(("seq", "head"), None))
    return jax.shard_map(
        on_device, mesh=mesh, in_specs=in_specs, out_specs=out_specs, check_vma=False
    )
```

```python
import functools

import jax
import jax.numpy as jnp
from jax import lax
from jax.experimental import pallas as pl
from jax.experimental.pallas import tpu as pltpu
from jax.sharding import PartitionSpec as P

MESH = pl.DeviceIdType.MESH
WIN = 2048
ROWS = 256
PIECE = 16
UNITS = 5
NY = 4
BAND = NY * PIECE
KEYS = 9 * BAND
PAD = 640
f32, bf16 = jnp.float32, jnp.bfloat16


def halves(value):
    high = value.astype(bf16)
    return high, (value - high.astype(f32)).astype(bf16)


def dot(a, b, b_dim):
    return lax.dot_general(a, b, (((1,), (b_dim,)), ((), ())), preferred_element_type=f32)


def dot3(a_high, a_low, b_high, b_low, b_dim):
    left = jnp.concatenate([a_high, a_high, a_low], axis=1)
    right = jnp.concatenate([b_high, b_low, b_high], axis=b_dim)
    return dot(left, right, b_dim)


def kernel(
    q_hbm, k_hbm, v_hbm, o_hbm, g_hbm, norm_hbm, ids_hbm,
    dq_hbm, dk_hbm, dv_hbm,
    dq_out, dk_out, dv_out, qb, gb, st, fwd, norm_in, ids_in, k_in, v_in,
    kbuf, vbuf, idq,
    kf, kh, kl, vh, vl, kth, ktl, bias,
    qh, ql, gh, gl, sh, sl,
    acc_k, acc_v, core_k, core_v, y_k, u_k, u_v, y_v, sum_k, sum_v, dq_part, dq_in,
    in_sem, out_sem, x_send, x_recv, k_send, k_recv, v_send, v_recv, c_send, c_recv, r_send, r_recv, u_send, u_recv, y_send, y_recv,
):
    seq, head = lax.axis_index("seq"), lax.axis_index("head")
    n_seq = lax.axis_size("seq")
    unit, core = lax.div(seq, 2), lax.rem(seq, 2)
    n_unit = n_seq // 2
    yh, x = lax.div(head, 4), lax.rem(head, 4)
    other = 1 - core

    def at_unit(d):
        return (lax.rem(unit + d + n_unit, n_unit) * 2 + core, head)

    def at_y(d):
        return (seq, lax.rem(yh + d, NY) * 4 + x)

    def at_x(d):
        return (seq, yh * 4 + lax.rem(x + d + 4, 4))

    partner = (unit * 2 + other, head)

    def send(src, dst, s_sem, r_sem, to):
        copy = pltpu.make_async_remote_copy(
            src_ref=src, dst_ref=dst, send_sem=s_sem, recv_sem=r_sem, device_id=to, device_id_type=MESH
        )
        copy.start()
        started.append(copy)
        return copy

    def landed(dst, r_sem):
        pltpu.make_async_remote_copy(
            src_ref=dst, dst_ref=dst, send_sem=r_sem, recv_sem=r_sem, device_id=partner, device_id_type=MESH
        ).wait_recv()

    started = []

    loads = [
        pltpu.make_async_copy(src, dst, in_sem.at[i])
        for i, (src, dst) in enumerate(
            (
                (q_hbm, qb.at[0]), (k_hbm, k_in), (v_hbm, v_in), (ids_hbm, ids_in),
                (g_hbm, gb.at[0]), (o_hbm, fwd), (norm_hbm, norm_in),
            )
        )
    ]
    for load in loads:
        load.start()
    barrier = pltpu.get_barrier_semaphore()
    greeted = [at_x(1), at_x(-1), at_x(2), partner]
    greeted += [at_y(d) for d in (1, 2, 3)] + [at_unit(-d) for d in (1, 2, 3, 4)]
    for device in greeted:
        pl.semaphore_signal(barrier, inc=1, device_id=device, device_id_type=MESH)

    for load in loads[:4]:
        load.wait()
    ids_row = ids_in[...].astype(f32)
    across = lax.broadcasted_iota(jnp.int32, (8, PIECE), 1)
    down = lax.broadcasted_iota(jnp.int32, (8, PIECE), 0)
    ids_low = jnp.sum(jnp.where(across == down, ids_row, 0.0), axis=1, keepdims=True)
    ids_high = jnp.sum(jnp.where(across == down + 8, ids_row, 0.0), axis=1, keepdims=True)
    lane = lax.broadcasted_iota(jnp.int32, (8, 128), 1)
    ids_tile = jnp.where(lane < 64, ids_low, ids_high)
    mine_k = kbuf.at[4, core, 0]
    mine_v = vbuf.at[4, core, 0]
    kbuf[4, core, 0, 0:16, :] = k_in[:, :128]
    kbuf[4, core, 0, 16:32, :] = k_in[:, 128:]
    kbuf[4, core, 0, 32:40, :] = ids_tile
    vbuf[4, core, 0, 0:16, :] = v_in[:, :128]
    vbuf[4, core, 0, 16:32, :] = v_in[:, 128:]
    pl.semaphore_wait(barrier, len(greeted))

    q_right = send(qb.at[0], qb.at[1], x_send.at[0], x_recv.at[0], at_x(1))
    q_left = send(qb.at[0], qb.at[2], x_send.at[1], x_recv.at[1], at_x(-1))
    for d in (1, 2, 3):
        send(mine_k, kbuf.at[4, core, 4 - d], k_send.at[d - 1], k_recv.at[3 - d], at_y(d))
    for d in (1, 2, 3, 4):
        send(mine_v, vbuf.at[4 - d, core, 0], v_send.at[d - 1], v_recv.at[d - 1], at_unit(d))
    for d in (1, 2, 3, 4):
        send(mine_k, kbuf.at[4 - d, core, 0], k_send.at[d + 2], k_recv.at[d + 2], at_unit(d))
    for d in (1, 2, 3):
        send(mine_v, vbuf.at[4, core, 4 - d], v_send.at[d + 3], v_recv.at[d + 3], at_y(d))

    for load in loads[4:]:
        load.wait()
    product = gb[0] * fwd[...]
    fwd[...] = product
    folded = fwd[pl.ds(0, ROWS, stride=2), :] + fwd[pl.ds(1, ROWS, stride=2), :]
    st[0, 0:1, :] = norm_in[...]
    st[0, 1:2, :] = jnp.sum(folded.T, axis=0, keepdims=True)
    st[0, 2:8, :] = jnp.zeros((6, ROWS), f32)

    for r in (1, 2, 3):
        landed(kbuf.at[4, core, r], k_recv.at[r - 1])
    along = pl.ds(1, 3)
    for d in (1, 2, 3, 4):
        send(kbuf.at[4, core, along], kbuf.at[4 - d, core, along], k_send.at[d + 6], k_recv.at[d + 6], at_unit(d))
    for d in (1, 2, 3, 4):
        landed(vbuf.at[4 - d, core, 0], v_recv.at[d - 1])
    past = pl.ds(0, 4)
    for d in (1, 2, 3):
        send(vbuf.at[past, core, 0], vbuf.at[past, core, 4 - d], v_send.at[d + 6], v_recv.at[d + 6], at_y(d))
    idq[pl.ds(x, 1)] = kbuf[4, core, :, 32:40, :][None]
    for d in (1, 2, 3):
        send(idq.at[x], idq.at[x], x_send.at[d + 9], x_recv.at[d + 9], at_x(d))
    q_right.wait_send()
    q_left.wait_send()
    started.remove(q_right)
    started.remove(q_left)
    send(gb.at[0], gb.at[1], x_send.at[2], x_recv.at[2], at_x(1))
    send(gb.at[0], gb.at[2], x_send.at[3], x_recv.at[3], at_x(-1))
    send(st.at[0], st.at[1], x_send.at[4], x_recv.at[4], at_x(1))
    send(st.at[0], st.at[2], x_send.at[5], x_recv.at[5], at_x(-1))
    landed(qb.at[1], x_recv.at[0])
    send(qb.at[1], qb.at[3], x_send.at[6], x_recv.at[6], at_x(1))

    for d in (1, 2, 3):
        landed(idq.at[lax.rem(x + 4 - d, 4)], x_recv.at[d + 9])
    pieces = []
    for y in range(NY):
        for col in range(4):
            tile = idq[col, lax.rem(y + NY - yh, NY)]
            pieces.append(jnp.broadcast_to(tile[:, 0:1], (8, 128)))
            pieces.append(jnp.broadcast_to(tile[:, 64:65], (8, 128)))
    ids_query = jnp.concatenate(pieces, axis=0).T[0:1, :]
    query_pos = core * ROWS + lax.broadcasted_iota(jnp.int32, (1, ROWS), 1)
    first = unit * 2 * ROWS
    row = lax.broadcasted_iota(jnp.int32, (BAND, 1), 0)
    row_pos = lax.rem(yh + row // PIECE, NY) * BAND + x * PIECE + row % PIECE

    def prepare(band, j, c):
        rows = slice(band * BAND, (band + 1) * BAND)

        def wide(ref, lo):
            return ref[j, c, :, lo : lo + PIECE, :].reshape(BAND, 128)

        keys = jnp.concatenate([wide(kbuf, 0), wide(kbuf, PIECE)], axis=1)
        vals = jnp.concatenate([wide(vbuf, 0), wide(vbuf, PIECE)], axis=1)
        kf[rows, :] = keys
        kh[rows, :], kl[rows, :] = halves(keys)
        vh[rows, :], vl[rows, :] = halves(vals)
        tiles = kbuf[j, c, :, 32:40, :]
        ids = jnp.concatenate([tiles[:, :, 0:1], tiles[:, :, 64:65]], axis=1).reshape(BAND, 1)
        key_pos = row_pos + (core + band - 8) * ROWS
        apart = query_pos - key_pos
        allowed = (apart >= 0) & (apart < WIN) & (ids == ids_query) & (key_pos + first >= 0)
        bias[rows, :] = jnp.where(allowed, 0.0, -1e30)

    kf[KEYS:PAD, :] = jnp.zeros((PAD - KEYS, 256), f32)
    sh[KEYS:PAD, :] = jnp.zeros((PAD - KEYS, ROWS), bf16)
    sl[KEYS:PAD, :] = jnp.zeros((PAD - KEYS, ROWS), bf16)

    near = pl.ds(other, 4)
    for d in (1, 2, 3):
        landed(vbuf.at[4, core, 4 - d], v_recv.at[d + 3])
        landed(vbuf.at[past, core, 4 - d], v_recv.at[d + 6])
    send(vbuf.at[near, core], vbuf.at[near, core], c_send.at[1], c_recv.at[1], partner)
    for d in (1, 2, 3, 4):
        landed(kbuf.at[4 - d, core, 0], k_recv.at[d + 2])
        landed(kbuf.at[4 - d, core, along], k_recv.at[d + 6])
    send(kbuf.at[near, core], kbuf.at[near, core], c_send.at[0], c_recv.at[0], partner)
    for j in range(UNITS):
        prepare(2 * j, j, core)
    landed(gb.at[2], x_recv.at[3])
    send(gb.at[2], gb.at[3], x_send.at[7], x_recv.at[7], at_x(-1))
    landed(st.at[1], x_recv.at[4])
    send(st.at[1], st.at[3], x_send.at[8], x_recv.at[8], at_x(1))
    landed(vbuf.at[pl.ds(core, 4), other], c_recv.at[1])
    landed(kbuf.at[pl.ds(core, 4), other], c_recv.at[0])
    for i in range(4):
        prepare(2 * i + 1, core + i, other)
    for i in range(PAD // 128):
        cols = slice(i * 128, (i + 1) * 128)
        kth[:, cols], ktl[:, cols] = halves(kf[cols, :].T)

    TILE = 576

    def one_head(slot, is_first):
        even, odd = pl.ds(0, ROWS, stride=2), pl.ds(1, ROWS, stride=2)
        qh[...], ql[...] = halves(jnp.concatenate([qb[slot, even, :], qb[slot, odd, :]], axis=1) * 0.0625)
        gh[...], gl[...] = halves(jnp.concatenate([gb[slot, even, :], gb[slot, odd, :]], axis=1))
        norm, delta = st[slot, 0:1, :], st[slot, 1:2, :]
        for t in range(KEYS // TILE):
            rows = slice(t * TILE, (t + 1) * TILE)
            scores = dot3(kh[rows, :], kl[rows, :], qh[...], ql[...], 1)
            grads = dot3(vh[rows, :], vl[rows, :], gh[...], gl[...], 1)
            probs = jnp.exp(scores - norm + bias[rows, :])
            grads = probs * (grads - delta)
            p_high, p_low = halves(probs)
            s_high, s_low = halves(grads)
            sh[rows, :] = s_high
            sl[rows, :] = s_low
            part_v = dot3(p_high, p_low, gh[...], gl[...], 0)
            part_k = dot3(s_high, s_low, qh[...], ql[...], 0)
            for i in range(TILE // BAND):
                block = core + t * (TILE // BAND) + i
                j, c = lax.div(block, 2), lax.rem(block, 2)
                part = slice(i * BAND, (i + 1) * BAND)
                if is_first:
                    acc_v[j, c] = part_v[part]
                    acc_k[j, c] = part_k[part]
                else:
                    acc_v[j, c] += part_v[part]
                    acc_k[j, c] += part_k[part]

    def head_queries(slot):
        dq_part[slot] = dot3(kth[...], ktl[...], sh[...], sl[...], 0)

    one_head(0, True)
    head_queries(0)
    landed(gb.at[1], x_recv.at[2])
    one_head(1, False)
    head_queries(1)
    send(dq_part.at[1], dq_in.at[0], x_send.at[13], x_recv.at[13], at_x(-1))
    landed(qb.at[2], x_recv.at[1])
    landed(st.at[2], x_recv.at[5])
    one_head(2, False)
    head_queries(2)
    send(dq_part.at[2], dq_in.at[1], x_send.at[14], x_recv.at[14], at_x(1))
    landed(qb.at[3], x_recv.at[6])
    landed(gb.at[3], x_recv.at[7])
    landed(st.at[3], x_recv.at[8])
    one_head(3, False)

    share = pl.ds(core, 4)
    send(acc_v.at[share, other], core_v, c_send.at[2], c_recv.at[2], partner)
    send(acc_k.at[share, other], core_k, c_send.at[3], c_recv.at[3], partner)
    head_queries(3)
    send(dq_part.at[3], dq_in.at[2], x_send.at[15], x_recv.at[15], at_x(2))

    def piece(r):
        return pl.ds(r * PIECE, PIECE)

    def values_on(r):
        for d in (4, 3, 2, 1):
            i = 4 * r + d - 1
            send(acc_v.at[4 - d, core, piece(r)], u_v.at[d - 1, piece(r)], u_send.at[i], u_recv.at[i], at_unit(-d))

    def keys_on(j):
        for r in (2, 1, 3):
            i = 3 * j + r - 1
            send(acc_k.at[j, core, piece(r)], y_k.at[r - 1, j], y_send.at[i], y_recv.at[i], at_y(r))

    def values_total(r):
        total = acc_v[4, core, piece(r)]
        for d in (4, 3, 2, 1):
            landed(u_v.at[d - 1, piece(r)], u_recv.at[4 * r + d - 1])
            total = total + u_v[d - 1, piece(r)]
        return total

    def keys_total(j):
        total = acc_k[j, core, :PIECE]
        for r in (2, 1, 3):
            landed(y_k.at[r - 1, j], y_recv.at[3 * j + r - 1])
            total = total + y_k[r - 1, j]
        return total

    landed(core_v, c_recv.at[2])
    for i in range(4):
        acc_v[other + i, core] += core_v[i]
    values_on(2)
    landed(core_k, c_recv.at[3])
    for i in range(4):
        acc_k[other + i, core] += core_k[i]
    keys_on(0)
    values_on(1)
    keys_on(1)
    values_on(3)
    keys_on(2)
    keys_on(3)
    values_on(0)
    keys_on(4)
    for r, j in ((2, 0), (1, 1), (3, 2), (None, 3)):
        if r is not None:
            sum_v[piece(r), :] = values_total(r)
            send(sum_v.at[piece(r)], y_v.at[r - 1], r_send.at[r - 1], r_recv.at[r - 1], at_y(r))
        sum_k[j] = keys_total(j)
        send(sum_k.at[j], u_k.at[3 - j], r_send.at[6 - j], r_recv.at[6 - j], at_unit(j - 4))

    for i in range(3):
        landed(dq_in.at[i], x_recv.at[13 + i])
    total_q = (dq_part[0] + dq_in[0] + dq_in[1] + dq_in[2]) * 0.0625
    total_q = total_q.T
    dq_out[pl.ds(0, ROWS, stride=2), :] = total_q[:, :128]
    dq_out[pl.ds(1, ROWS, stride=2), :] = total_q[:, 128:]
    stores = [pltpu.make_async_copy(dq_out, dq_hbm, out_sem.at[0])]
    stores[0].start()

    total = values_total(0)
    for r in (1, 2, 3):
        landed(y_v.at[r - 1], r_recv.at[r - 1])
        total = total + y_v[r - 1]
    dv_out[...] = total
    stores.append(pltpu.make_async_copy(dv_out, dv_hbm, out_sem.at[1]))
    stores[1].start()
    total = keys_total(4)
    for d in (1, 2, 3, 4):
        landed(u_k.at[d - 1], r_recv.at[d + 2])
        total = total + u_k[d - 1]
    dk_out[...] = total
    stores.append(pltpu.make_async_copy(dk_out, dk_hbm, out_sem.at[2]))
    stores[2].start()
    for store in stores:
        store.wait()
    for copy in started:
        copy.wait_send()


def hand_over(dq_in, dk_in, dv_in, dq_out, dk_out, dv_out):
    dq_out[...] = dq_in[...]
    dk_out[...] = dk_in[...]
    dv_out[...] = dv_in[...]


def on_device(queries, key_rows, value_rows, forward_out, out_grad, log_norm, doc_ids):
    flat = (2 * ROWS, 128)
    vmem, dma = pltpu.VMEM, pltpu.SemaphoreType.DMA
    dq, dk, dv = pl.pallas_call(
        kernel,
        out_shape=(
            jax.ShapeDtypeStruct(flat, f32),
            jax.ShapeDtypeStruct((PIECE, 256), f32),
            jax.ShapeDtypeStruct((PIECE, 256), f32),
        ),
        in_specs=[pl.BlockSpec(memory_space=pl.ANY)] * 7,
        out_specs=(pl.BlockSpec(memory_space=pl.ANY),) * 3,
        scratch_shapes=[
            vmem(flat, f32), vmem((PIECE, 256), f32), vmem((PIECE, 256), f32),
            vmem((4, *flat), f32), vmem((4, *flat), f32), vmem((4, 8, ROWS), f32), vmem(flat, f32),
            vmem((1, ROWS), f32), vmem((1, PIECE), jnp.int32), vmem((PIECE, 256), f32), vmem((PIECE, 256), f32),
            vmem((UNITS, 2, NY, 40, 128), f32), vmem((UNITS, 2, NY, 32, 128), f32), vmem((4, NY, 8, 128), f32),
            vmem((PAD, 256), f32), vmem((KEYS, 256), bf16), vmem((KEYS, 256), bf16),
            vmem((KEYS, 256), bf16), vmem((KEYS, 256), bf16), vmem((256, PAD), bf16), vmem((256, PAD), bf16),
            vmem((KEYS, ROWS), f32),
            vmem((ROWS, 256), bf16), vmem((ROWS, 256), bf16), vmem((ROWS, 256), bf16), vmem((ROWS, 256), bf16),
            vmem((PAD, ROWS), bf16), vmem((PAD, ROWS), bf16),
            vmem((UNITS, 2, BAND, 256), f32), vmem((UNITS, 2, BAND, 256), f32),
            vmem((4, BAND, 256), f32), vmem((4, BAND, 256), f32),
            vmem((3, UNITS, PIECE, 256), f32), vmem((4, PIECE, 256), f32), vmem((4, BAND, 256), f32),
            vmem((3, PIECE, 256), f32), vmem((UNITS, PIECE, 256), f32), vmem((BAND, 256), f32),
            vmem((4, 256, ROWS), f32), vmem((3, 256, ROWS), f32),
            dma((7,)), dma((3,)), dma((16,)), dma((16,)), dma((11,)), dma((11,)), dma((10,)), dma((10,)),
            dma((4,)), dma((4,)), dma((7,)), dma((7,)), dma((16,)), dma((16,)), dma((15,)), dma((15,)),
        ],
        compiler_params=pltpu.CompilerParams(
            collective_id=0, has_side_effects=True, vmem_limit_bytes=60 * 2**20
        ),
    )(
        queries.reshape(flat), key_rows, value_rows, forward_out.reshape(flat), out_grad.reshape(flat),
        log_norm.reshape(1, ROWS), doc_ids.reshape(1, PIECE),
    )
    dq, dk, dv = pl.pallas_call(
        hand_over,
        out_shape=tuple(jax.ShapeDtypeStruct(a.shape, a.dtype) for a in (dq, dk, dv)),
        in_specs=[pl.BlockSpec(memory_space=pltpu.VMEM)] * 3,
        out_specs=(pl.BlockSpec(memory_space=pltpu.VMEM),) * 3,
    )(dq, dk, dv)
    return dq.reshape(ROWS, 1, 256), dk, dv


def solution(mesh):
    in_specs = (
        P("seq", "head", None),
        P(("seq", "head"), None),
        P(("seq", "head"), None),
        P("seq", "head", None),
        P("seq", "head", None),
        P("seq", "head"),
        P(("seq", "head")),
    )
    out_specs = (P("seq", "head", None), P(("seq", "head"), None), P(("seq", "head"), None))
    return jax.shard_map(
        on_device, mesh=mesh, in_specs=in_specs, out_specs=out_specs, check_vma=False
    )
```

```python
import functools

import jax
import jax.numpy as jnp
from jax import lax
from jax.experimental import pallas as pl
from jax.experimental.pallas import tpu as pltpu
from jax.sharding import PartitionSpec as P

MESH = pl.DeviceIdType.MESH
WIN = 2048
ROWS = 256
PIECE = 16
UNITS = 5
NY = 4
BAND = NY * PIECE
KEYS = 9 * BAND
PAD = 640
f32, bf16 = jnp.float32, jnp.bfloat16


def halves(value):
    high = value.astype(bf16)
    return high, (value - high.astype(f32)).astype(bf16)


def dot(a, b, b_dim):
    return lax.dot_general(a, b, (((1,), (b_dim,)), ((), ())), preferred_element_type=f32)


def dot3(a_high, a_low, b_high, b_low, b_dim):
    left = jnp.concatenate([a_high, a_high, a_low], axis=1)
    right = jnp.concatenate([b_high, b_low, b_high], axis=b_dim)
    return dot(left, right, b_dim)


def kernel(
    q_hbm, k_hbm, v_hbm, o_hbm, g_hbm, norm_hbm, ids_hbm,
    dq_hbm, dk_hbm, dv_hbm,
    dq_out, dk_out, dv_out, qb, gb, st, fwd, norm_in, ids_in, k_in, v_in,
    kbuf, vbuf, idq,
    kf, kh, kl, vh, vl, kth, ktl, bias,
    qh, ql, gh, gl, sh, sl,
    acc_k, acc_v, core_k, core_v, y_k, u_k, u_v, y_v, sum_k, sum_v, dq_part, dq_in,
    in_sem, out_sem, x_send, x_recv, k_send, k_recv, v_send, v_recv, c_send, c_recv, r_send, r_recv, u_send, u_recv, y_send, y_recv,
):
    seq, head = lax.axis_index("seq"), lax.axis_index("head")
    n_seq = lax.axis_size("seq")
    unit, core = lax.div(seq, 2), lax.rem(seq, 2)
    n_unit = n_seq // 2
    yh, x = lax.div(head, 4), lax.rem(head, 4)
    other = 1 - core

    def at_unit(d):
        return (lax.rem(unit + d + n_unit, n_unit) * 2 + core, head)

    def at_y(d):
        return (seq, lax.rem(yh + d, NY) * 4 + x)

    def at_x(d):
        return (seq, yh * 4 + lax.rem(x + d + 4, 4))

    partner = (unit * 2 + other, head)

    def send(src, dst, s_sem, r_sem, to):
        copy = pltpu.make_async_remote_copy(
            src_ref=src, dst_ref=dst, send_sem=s_sem, recv_sem=r_sem, device_id=to, device_id_type=MESH
        )
        copy.start()
        started.append(copy)
        return copy

    def landed(dst, r_sem):
        pltpu.make_async_remote_copy(
            src_ref=dst, dst_ref=dst, send_sem=r_sem, recv_sem=r_sem, device_id=partner, device_id_type=MESH
        ).wait_recv()

    started = []

    loads = [
        pltpu.make_async_copy(src, dst, in_sem.at[i])
        for i, (src, dst) in enumerate(
            (
                (q_hbm, qb.at[0]), (k_hbm, k_in), (v_hbm, v_in), (ids_hbm, ids_in),
                (g_hbm, gb.at[0]), (o_hbm, fwd), (norm_hbm, norm_in),
            )
        )
    ]
    for load in loads:
        load.start()
    barrier = pltpu.get_barrier_semaphore()
    greeted = [at_x(1), at_x(-1), at_x(2), partner]
    greeted += [at_y(d) for d in (1, 2, 3)] + [at_unit(-d) for d in (1, 2, 3, 4)]
    for device in greeted:
        pl.semaphore_signal(barrier, inc=1, device_id=device, device_id_type=MESH)

    for load in loads[:4]:
        load.wait()
    ids_row = ids_in[...].astype(f32)
    across = lax.broadcasted_iota(jnp.int32, (8, PIECE), 1)
    down = lax.broadcasted_iota(jnp.int32, (8, PIECE), 0)
    ids_low = jnp.sum(jnp.where(across == down, ids_row, 0.0), axis=1, keepdims=True)
    ids_high = jnp.sum(jnp.where(across == down + 8, ids_row, 0.0), axis=1, keepdims=True)
    lane = lax.broadcasted_iota(jnp.int32, (8, 128), 1)
    ids_tile = jnp.where(lane < 64, ids_low, ids_high)
    mine_k = kbuf.at[4, core, 0]
    mine_v = vbuf.at[4, core, 0]
    kbuf[4, core, 0, 0:16, :] = k_in[:, :128]
    kbuf[4, core, 0, 16:32, :] = k_in[:, 128:]
    kbuf[4, core, 0, 32:40, :] = ids_tile
    vbuf[4, core, 0, 0:16, :] = v_in[:, :128]
    vbuf[4, core, 0, 16:32, :] = v_in[:, 128:]
    pl.semaphore_wait(barrier, len(greeted))

    q_right = send(qb.at[0], qb.at[1], x_send.at[0], x_recv.at[0], at_x(1))
    q_left = send(qb.at[0], qb.at[2], x_send.at[1], x_recv.at[1], at_x(-1))
    for d in (1, 2, 3):
        send(mine_k, kbuf.at[4, core, 4 - d], k_send.at[d - 1], k_recv.at[3 - d], at_y(d))
    for d in (1, 2, 3, 4):
        send(mine_v, vbuf.at[4 - d, core, 0], v_send.at[d - 1], v_recv.at[d - 1], at_unit(d))
    for d in (1, 2, 3, 4):
        send(mine_k, kbuf.at[4 - d, core, 0], k_send.at[d + 2], k_recv.at[d + 2], at_unit(d))
    for d in (1, 2, 3):
        send(mine_v, vbuf.at[4, core, 4 - d], v_send.at[d + 3], v_recv.at[d + 3], at_y(d))

    for load in loads[4:]:
        load.wait()
    product = gb[0] * fwd[...]
    fwd[...] = product
    folded = fwd[pl.ds(0, ROWS, stride=2), :] + fwd[pl.ds(1, ROWS, stride=2), :]
    st[0, 0:1, :] = norm_in[...]
    st[0, 1:2, :] = jnp.sum(folded.T, axis=0, keepdims=True)
    st[0, 2:8, :] = jnp.zeros((6, ROWS), f32)

    for r in (1, 2, 3):
        landed(kbuf.at[4, core, r], k_recv.at[r - 1])
    along = pl.ds(1, 3)
    for d in (1, 2, 3, 4):
        send(kbuf.at[4, core, along], kbuf.at[4 - d, core, along], k_send.at[d + 6], k_recv.at[d + 6], at_unit(d))
    for d in (1, 2, 3, 4):
        landed(vbuf.at[4 - d, core, 0], v_recv.at[d - 1])
    past = pl.ds(0, 4)
    for d in (1, 2, 3):
        send(vbuf.at[past, core, 0], vbuf.at[past, core, 4 - d], v_send.at[d + 6], v_recv.at[d + 6], at_y(d))
    idq[pl.ds(x, 1)] = kbuf[4, core, :, 32:40, :][None]
    for d in (1, 2, 3):
        send(idq.at[x], idq.at[x], x_send.at[d + 9], x_recv.at[d + 9], at_x(d))
    q_right.wait_send()
    q_left.wait_send()
    started.remove(q_right)
    started.remove(q_left)
    send(gb.at[0], gb.at[1], x_send.at[2], x_recv.at[2], at_x(1))
    send(gb.at[0], gb.at[2], x_send.at[3], x_recv.at[3], at_x(-1))
    send(st.at[0], st.at[1], x_send.at[4], x_recv.at[4], at_x(1))
    send(st.at[0], st.at[2], x_send.at[5], x_recv.at[5], at_x(-1))
    landed(qb.at[1], x_recv.at[0])
    send(qb.at[1], qb.at[3], x_send.at[6], x_recv.at[6], at_x(1))

    def split(slot):
        even, odd = pl.ds(0, ROWS, stride=2), pl.ds(1, ROWS, stride=2)
        qh[...], ql[...] = halves(jnp.concatenate([qb[slot, even, :], qb[slot, odd, :]], axis=1) * 0.0625)
        gh[...], gl[...] = halves(jnp.concatenate([gb[slot, even, :], gb[slot, odd, :]], axis=1))

    split(0)

    for d in (1, 2, 3):
        landed(idq.at[lax.rem(x + 4 - d, 4)], x_recv.at[d + 9])
    pieces = []
    for y in range(NY):
        for col in range(4):
            tile = idq[col, lax.rem(y + NY - yh, NY)]
            pieces.append(jnp.broadcast_to(tile[:, 0:1], (8, 128)))
            pieces.append(jnp.broadcast_to(tile[:, 64:65], (8, 128)))
    ids_query = jnp.concatenate(pieces, axis=0).T[0:1, :]
    query_pos = core * ROWS + lax.broadcasted_iota(jnp.int32, (1, ROWS), 1)
    first = unit * 2 * ROWS
    row = lax.broadcasted_iota(jnp.int32, (BAND, 1), 0)
    row_pos = lax.rem(yh + row // PIECE, NY) * BAND + x * PIECE + row % PIECE

    def prepare(band, j, c):
        rows = slice(band * BAND, (band + 1) * BAND)

        def wide(ref, lo):
            return ref[j, c, :, lo : lo + PIECE, :].reshape(BAND, 128)

        keys = jnp.concatenate([wide(kbuf, 0), wide(kbuf, PIECE)], axis=1)
        vals = jnp.concatenate([wide(vbuf, 0), wide(vbuf, PIECE)], axis=1)
        kf[rows, :] = keys
        kh[rows, :], kl[rows, :] = halves(keys)
        vh[rows, :], vl[rows, :] = halves(vals)
        tiles = kbuf[j, c, :, 32:40, :]
        ids = jnp.concatenate([tiles[:, :, 0:1], tiles[:, :, 64:65]], axis=1).reshape(BAND, 1)
        key_pos = row_pos + (core + band - 8) * ROWS
        apart = query_pos - key_pos
        allowed = (apart >= 0) & (apart < WIN) & (ids == ids_query) & (key_pos + first >= 0)
        bias[rows, :] = jnp.where(allowed, 0.0, -1e30)

    kf[KEYS:PAD, :] = jnp.zeros((PAD - KEYS, 256), f32)
    sh[:, KEYS:PAD, :] = jnp.zeros((4, PAD - KEYS, ROWS), bf16)
    sl[:, KEYS:PAD, :] = jnp.zeros((4, PAD - KEYS, ROWS), bf16)

    near = pl.ds(other, 4)
    for d in (1, 2, 3):
        landed(vbuf.at[4, core, 4 - d], v_recv.at[d + 3])
        landed(vbuf.at[past, core, 4 - d], v_recv.at[d + 6])
    send(vbuf.at[near, core], vbuf.at[near, core], c_send.at[1], c_recv.at[1], partner)
    for d in (1, 2, 3, 4):
        landed(kbuf.at[4 - d, core, 0], k_recv.at[d + 2])
        landed(kbuf.at[4 - d, core, along], k_recv.at[d + 6])
    send(kbuf.at[near, core], kbuf.at[near, core], c_send.at[0], c_recv.at[0], partner)
    for j in range(UNITS):
        prepare(2 * j, j, core)
    landed(gb.at[2], x_recv.at[3])
    send(gb.at[2], gb.at[3], x_send.at[7], x_recv.at[7], at_x(-1))
    landed(st.at[1], x_recv.at[4])
    send(st.at[1], st.at[3], x_send.at[8], x_recv.at[8], at_x(1))
    landed(vbuf.at[pl.ds(core, 4), other], c_recv.at[1])
    landed(kbuf.at[pl.ds(core, 4), other], c_recv.at[0])
    for i in range(4):
        prepare(2 * i + 1, core + i, other)
    for i in range(PAD // 128):
        cols = slice(i * 128, (i + 1) * 128)
        kth[:, cols], ktl[:, cols] = halves(kf[cols, :].T)

    TILE = 576

    def one_head(slot, is_first):
        if slot:
            split(slot)
        norm, delta = st[slot, 0:1, :], st[slot, 1:2, :]
        for t in range(KEYS // TILE):
            rows = slice(t * TILE, (t + 1) * TILE)
            scores = dot3(kh[rows, :], kl[rows, :], qh[...], ql[...], 1)
            grads = dot3(vh[rows, :], vl[rows, :], gh[...], gl[...], 1)
            probs = jnp.exp(scores - norm + bias[rows, :])
            grads = probs * (grads - delta)
            p_high, p_low = halves(probs)
            s_high, s_low = halves(grads)
            sh[slot, rows, :] = s_high
            sl[slot, rows, :] = s_low
            part_v = dot3(p_high, p_low, gh[...], gl[...], 0)
            part_k = dot3(s_high, s_low, qh[...], ql[...], 0)
            for i in range(TILE // BAND):
                block = core + t * (TILE // BAND) + i
                j, c = lax.div(block, 2), lax.rem(block, 2)
                part = slice(i * BAND, (i + 1) * BAND)
                if is_first:
                    acc_v[j, c] = part_v[part]
                    acc_k[j, c] = part_k[part]
                else:
                    acc_v[j, c] += part_v[part]
                    acc_k[j, c] += part_k[part]

    def head_queries(slot):
        dq_part[slot] = dot3(kth[...], ktl[...], sh[slot], sl[slot], 0)

    one_head(0, True)
    landed(gb.at[1], x_recv.at[2])
    one_head(1, False)
    head_queries(1)
    send(dq_part.at[1], dq_in.at[0], x_send.at[13], x_recv.at[13], at_x(-1))
    landed(qb.at[2], x_recv.at[1])
    landed(st.at[2], x_recv.at[5])
    one_head(2, False)
    head_queries(2)
    send(dq_part.at[2], dq_in.at[1], x_send.at[14], x_recv.at[14], at_x(1))
    landed(qb.at[3], x_recv.at[6])
    landed(gb.at[3], x_recv.at[7])
    landed(st.at[3], x_recv.at[8])
    one_head(3, False)

    share = pl.ds(core, 4)
    send(acc_v.at[share, other], core_v, c_send.at[2], c_recv.at[2], partner)
    send(acc_k.at[share, other], core_k, c_send.at[3], c_recv.at[3], partner)
    head_queries(3)
    send(dq_part.at[3], dq_in.at[2], x_send.at[15], x_recv.at[15], at_x(2))

    def piece(r):
        return pl.ds(r * PIECE, PIECE)

    def values_on(r):
        for d in (4, 3, 2, 1):
            i = 4 * r + d - 1
            send(acc_v.at[4 - d, core, piece(r)], u_v.at[d - 1, piece(r)], u_send.at[i], u_recv.at[i], at_unit(-d))

    def keys_on(j):
        for r in (2, 1, 3):
            i = 3 * j + r - 1
            send(acc_k.at[j, core, piece(r)], y_k.at[r - 1, j], y_send.at[i], y_recv.at[i], at_y(r))

    def values_total(r):
        total = acc_v[4, core, piece(r)]
        for d in (4, 3, 2, 1):
            landed(u_v.at[d - 1, piece(r)], u_recv.at[4 * r + d - 1])
            total = total + u_v[d - 1, piece(r)]
        return total

    def keys_total(j):
        total = acc_k[j, core, :PIECE]
        for r in (2, 1, 3):
            landed(y_k.at[r - 1, j], y_recv.at[3 * j + r - 1])
            total = total + y_k[r - 1, j]
        return total

    landed(core_v, c_recv.at[2])
    for i in range(4):
        acc_v[other + i, core] += core_v[i]
    values_on(2)
    landed(core_k, c_recv.at[3])
    for i in range(4):
        acc_k[other + i, core] += core_k[i]
    keys_on(0)
    values_on(1)
    keys_on(1)
    values_on(3)
    keys_on(2)
    keys_on(3)
    values_on(0)
    keys_on(4)
    head_queries(0)
    for r, j in ((2, 0), (1, 1), (3, 2), (None, 3)):
        if r is not None:
            sum_v[piece(r), :] = values_total(r)
            send(sum_v.at[piece(r)], y_v.at[r - 1], r_send.at[r - 1], r_recv.at[r - 1], at_y(r))
        sum_k[j] = keys_total(j)
        send(sum_k.at[j], u_k.at[3 - j], r_send.at[6 - j], r_recv.at[6 - j], at_unit(j - 4))

    for i in range(3):
        landed(dq_in.at[i], x_recv.at[13 + i])
    total_q = (dq_part[0] + dq_in[0] + dq_in[1] + dq_in[2]) * 0.0625
    total_q = total_q.T
    dq_out[pl.ds(0, ROWS, stride=2), :] = total_q[:, :128]
    dq_out[pl.ds(1, ROWS, stride=2), :] = total_q[:, 128:]
    stores = [pltpu.make_async_copy(dq_out, dq_hbm, out_sem.at[0])]
    stores[0].start()

    total = values_total(0)
    for r in (1, 2, 3):
        landed(y_v.at[r - 1], r_recv.at[r - 1])
        total = total + y_v[r - 1]
    dv_out[...] = total
    stores.append(pltpu.make_async_copy(dv_out, dv_hbm, out_sem.at[1]))
    stores[1].start()
    total = keys_total(4)
    for d in (1, 2, 3, 4):
        landed(u_k.at[d - 1], r_recv.at[d + 2])
        total = total + u_k[d - 1]
    dk_out[...] = total
    stores.append(pltpu.make_async_copy(dk_out, dk_hbm, out_sem.at[2]))
    stores[2].start()
    for store in stores:
        store.wait()
    for copy in started:
        copy.wait_send()


def hand_over(dq_in, dk_in, dv_in, dq_out, dk_out, dv_out):
    dq_out[...] = dq_in[...]
    dk_out[...] = dk_in[...]
    dv_out[...] = dv_in[...]


def on_device(queries, key_rows, value_rows, forward_out, out_grad, log_norm, doc_ids):
    flat = (2 * ROWS, 128)
    vmem, dma = pltpu.VMEM, pltpu.SemaphoreType.DMA
    dq, dk, dv = pl.pallas_call(
        kernel,
        out_shape=(
            jax.ShapeDtypeStruct(flat, f32),
            jax.ShapeDtypeStruct((PIECE, 256), f32),
            jax.ShapeDtypeStruct((PIECE, 256), f32),
        ),
        in_specs=[pl.BlockSpec(memory_space=pl.ANY)] * 7,
        out_specs=(pl.BlockSpec(memory_space=pl.ANY),) * 3,
        scratch_shapes=[
            vmem(flat, f32), vmem((PIECE, 256), f32), vmem((PIECE, 256), f32),
            vmem((4, *flat), f32), vmem((4, *flat), f32), vmem((4, 8, ROWS), f32), vmem(flat, f32),
            vmem((1, ROWS), f32), vmem((1, PIECE), jnp.int32), vmem((PIECE, 256), f32), vmem((PIECE, 256), f32),
            vmem((UNITS, 2, NY, 40, 128), f32), vmem((UNITS, 2, NY, 32, 128), f32), vmem((4, NY, 8, 128), f32),
            vmem((PAD, 256), f32), vmem((KEYS, 256), bf16), vmem((KEYS, 256), bf16),
            vmem((KEYS, 256), bf16), vmem((KEYS, 256), bf16), vmem((256, PAD), bf16), vmem((256, PAD), bf16),
            vmem((KEYS, ROWS), f32),
            vmem((ROWS, 256), bf16), vmem((ROWS, 256), bf16), vmem((ROWS, 256), bf16), vmem((ROWS, 256), bf16),
            vmem((4, PAD, ROWS), bf16), vmem((4, PAD, ROWS), bf16),
            vmem((UNITS, 2, BAND, 256), f32), vmem((UNITS, 2, BAND, 256), f32),
            vmem((4, BAND, 256), f32), vmem((4, BAND, 256), f32),
            vmem((3, UNITS, PIECE, 256), f32), vmem((4, PIECE, 256), f32), vmem((4, BAND, 256), f32),
            vmem((3, PIECE, 256), f32), vmem((UNITS, PIECE, 256), f32), vmem((BAND, 256), f32),
            vmem((4, 256, ROWS), f32), vmem((3, 256, ROWS), f32),
            dma((7,)), dma((3,)), dma((16,)), dma((16,)), dma((11,)), dma((11,)), dma((10,)), dma((10,)),
            dma((4,)), dma((4,)), dma((7,)), dma((7,)), dma((16,)), dma((16,)), dma((15,)), dma((15,)),
        ],
        compiler_params=pltpu.CompilerParams(
            collective_id=0, has_side_effects=True, vmem_limit_bytes=60 * 2**20
        ),
    )(
        queries.reshape(flat), key_rows, value_rows, forward_out.reshape(flat), out_grad.reshape(flat),
        log_norm.reshape(1, ROWS), doc_ids.reshape(1, PIECE),
    )
    dq, dk, dv = pl.pallas_call(
        hand_over,
        out_shape=tuple(jax.ShapeDtypeStruct(a.shape, a.dtype) for a in (dq, dk, dv)),
        in_specs=[pl.BlockSpec(memory_space=pltpu.VMEM)] * 3,
        out_specs=(pl.BlockSpec(memory_space=pltpu.VMEM),) * 3,
    )(dq, dk, dv)
    return dq.reshape(ROWS, 1, 256), dk, dv


def solution(mesh):
    in_specs = (
        P("seq", "head", None),
        P(("seq", "head"), None),
        P(("seq", "head"), None),
        P("seq", "head", None),
        P("seq", "head", None),
        P("seq", "head"),
        P(("seq", "head")),
    )
    out_specs = (P("seq", "head", None), P(("seq", "head"), None), P(("seq", "head"), None))
    return jax.shard_map(
        on_device, mesh=mesh, in_specs=in_specs, out_specs=out_specs, check_vma=False
    )
```
